32 devices in a mesh: groups: 2 (over x), pair: 16 (over z, y, core).
Axes of the slice: x: 2, y: 2, z: 4, core: 2. Of those that a mesh axis runs over, the one named last changes fastest.
Arguments:
- t2_amp: float32 [128, 8, 9216], P(('groups', 'pair')), parts along dimension 0, may hold values from -6 to 6
- ladder_ints: bfloat16 [147456, 9216], P(('groups', 'pair')), parts along dimension 0, may hold values from -0.0625 to 0.0625
- fock_vv: float32 [16, 96, 96], P('groups'), parts along dimension 0, may hold values from -0.625 to 0.625
- vir_energy: float32 [16, 96], P('groups'), parts along dimension 0, may hold values from 0.5 to 4
- occ_energy: float32 [300], P('groups'), parts along dimension 0, may hold values from -3 to -0.5
- vir_sizes: int32 [16], P('groups'), parts along dimension 0, may hold values from 48 to 96, as said below
- pair_index: int32 [128, 2], P(('groups', 'pair')), parts along dimension 0, may hold values from 0 to 149, as said below
Outputs:
- increment: float32 [128, 8, 9216], P(('groups', 'pair')), parts along dimension 0
The draws below stay inside these ranges and needn't reach their ends.
There are 2 independent parts, one for each index of `groups`. The reference program is written for one: setup_inputs(seed, part) draws one part's arguments, and reference() takes and returns one part's arrays. A program takes and returns all parts, laid end to end along the dimension named above; each array names one. Nothing has to cross between parts.
Inputs may be any that keep to these rules, and one draw needn't show every extreme that they name: `vir_sizes`: at least one irrep block is full. `pair_index`: each pair has i <= j.
All inputs are finite; a program needn't handle non-finite values.
Results may differ from the reference program's by a relative error of at most 0.0016.
Values may be sent and summed in bfloat16 or wider, within the bound.
No kernel may reach another device: no remote copies, remote signals or barrier semaphores. Data moves between devices by JAX's collectives and lax.ppermute only.
A program may use at most 192 MiB of HBM per device.

```python
import math
import jax
import jax.numpy as jnp
from jax import lax

IRREPS = 8
VIRT_BLOCK = 96
OCC = 150
PAIRS = 64


def draw_vir_sizes(key, part):
    key = jax.random.fold_in(key, 11)
    first_key, second_key = jax.random.split(key)
    drawn = jax.random.randint(first_key, (IRREPS,), VIRT_BLOCK // 2, VIRT_BLOCK + 1)
    chosen = jax.random.randint(second_key, (), 0, IRREPS)
    return jnp.where(jnp.arange(IRREPS) == chosen, VIRT_BLOCK, drawn).astype(jnp.int32)


def draw_pair_index(key, part):
    key = jax.random.fold_in(key, 23)
    first_key, second_key, third_key = jax.random.split(key, 3)
    orbital_one = jax.random.randint(first_key, (PAIRS,), 0, OCC)
    orbital_two = jax.random.randint(second_key, (PAIRS,), 0, OCC)
    smaller = jnp.minimum(orbital_one, orbital_two)
    larger = jnp.maximum(orbital_one, orbital_two)
    chosen = jax.random.randint(third_key, (), 0, PAIRS)
    marked = jnp.arange(PAIRS) == chosen
    smaller = jnp.where(marked, 0, smaller)
    larger = jnp.where(marked, OCC - 1, larger)
    return jnp.stack([smaller, larger], axis=1).astype(jnp.int32)


def steps_of(own_key, dims, pieces, least, high):
    level, own = 1.0, jax.random.fold_in(own_key, 6)
    for position, shards_of in pieces:
        draws = jnp.exp(jax.random.uniform(jax.random.fold_in(own, position), (shards_of,), jnp.float32, least / len(pieces), high / len(pieces)))
        level = level * jnp.repeat(draws, dims[position] // shards_of).reshape([-1 if axis == position else 1 for axis in range(len(dims))])
    return level


def normal_values(own_key, shape, width, reach, pieces=(), held_as=jnp.bfloat16):
    gain = steps_of(own_key, shape, pieces, -0.22, 0.18) if pieces else 1.0
    entries = jax.random.normal(own_key, shape, jnp.float32) * width * gain
    return jnp.minimum(jnp.maximum(entries, -reach), reach).astype(held_as)


def setup_inputs(seed: int = 0, part: int = 0) -> dict:
    seeds = jax.random.split(jax.random.key(seed), 8)
    part_splits = jax.random.split(jax.random.fold_in(seeds[7], part), 8)
    return {
        "t2_amp": normal_values(part_splits[0], (PAIRS, IRREPS, VIRT_BLOCK * VIRT_BLOCK), 1.0, 6.0, ((0, 16),), jnp.float32),
        "ladder_ints": normal_values(part_splits[1], (IRREPS * VIRT_BLOCK * VIRT_BLOCK, VIRT_BLOCK * VIRT_BLOCK), (VIRT_BLOCK * VIRT_BLOCK) ** -0.5, 0.0625, ((0, 16),)),
        "fock_vv": normal_values(part_splits[2], (IRREPS, VIRT_BLOCK, VIRT_BLOCK), VIRT_BLOCK ** -0.5, 0.625, (), jnp.float32),
        "vir_energy": jnp.clip(jnp.exp(jax.random.uniform(part_splits[3], (IRREPS, VIRT_BLOCK), jnp.float32, math.log(0.5), math.log(4.0))), 0.5, 4.0),
        "occ_energy": jnp.clip(jax.random.uniform(part_splits[4], (OCC,), jnp.float32, -3.0, -0.5), -3.0, -0.5),
        "vir_sizes": draw_vir_sizes(jax.random.fold_in(jax.random.fold_in(seeds[7], part), 71), part),
        "pair_index": draw_pair_index(jax.random.fold_in(jax.random.fold_in(seeds[7], part), 71), part),
    }


def reference(t2_amp, ladder_ints, fock_vv, vir_energy, occ_energy, vir_sizes, pair_index):
    square = VIRT_BLOCK * VIRT_BLOCK
    live = jnp.arange(VIRT_BLOCK, dtype=jnp.int32)[None, :] < vir_sizes[:, None]
    pair_live = (live[:, :, None] & live[:, None, :]).reshape(IRREPS, square)
    masked = jnp.where(pair_live[None], t2_amp, jnp.zeros_like(t2_amp))
    block = masked[:, 0, :].astype(jnp.bfloat16)
    ladder = lax.dot_general(block, ladder_ints, (((1,), (1,)), ((), ())), preferred_element_type=jnp.float32)
    ladder = ladder.reshape(PAIRS, IRREPS, square)
    amps = masked.reshape(PAIRS, IRREPS, VIRT_BLOCK, VIRT_BLOCK)
    fock = jnp.einsum("phac,hcb->phab", amps, fock_vv, precision=lax.Precision.HIGHEST)
    fock = fock + jnp.einsum("hac,phcb->phab", fock_vv, amps, precision=lax.Precision.HIGHEST)
    fock = fock.reshape(PAIRS, IRREPS, square)
    matched = pair_index[:, :, None] == jnp.arange(OCC, dtype=jnp.int32)[None, None, :]
    chosen = jnp.sum(jnp.where(matched, occ_energy[None, None, :], jnp.zeros_like(occ_energy)[None, None, :]), axis=-1)
    vir_pair = (vir_energy[:, :, None] + vir_energy[:, None, :]).reshape(IRREPS, square)
    denom = vir_pair[None] - (chosen[:, 0] + chosen[:, 1])[:, None, None]
    total = (ladder + fock) / denom
    return jnp.where(pair_live[None], total, jnp.zeros_like(total))
```

```python
import functools

import jax
import jax.numpy as jnp
from jax import lax
from jax.experimental import pallas as pl
from jax.experimental.pallas import tpu as pltpu
from jax.sharding import PartitionSpec as P

CONTRACT_LAST = (((1,), (1,)), ((), ()))
VMEM_BYTES = 48 * 1024 * 1024


def tile_of(rows, most):
    for size in range(most - most % 128, 0, -128):
        if rows % size == 0:
            return size
    return rows


def pairs_by_core(own_ref, other_ref, amps):
    core = lax.rem(lax.axis_index("pair"), 2)
    count = own_ref.shape[0] * own_ref.shape[1]
    for ref, place in ((own_ref, core), (other_ref, 1 - core)):
        values = ref[...].astype(jnp.float32).reshape(count, ref.shape[2])
        amps[pl.ds(pl.multiple_of(place * count, count), count), :] = values.astype(amps.dtype)


def first_half_kernel(own_ref, other_ref, ints_ref, out_ref, amps):
    @pl.when(pl.program_id(0) == 0)
    def _():
        pairs_by_core(own_ref, other_ref, amps)

    out_ref[...] = lax.dot_general(
        ints_ref[...], amps[...], CONTRACT_LAST, preferred_element_type=jnp.float32
    ).T


def first_half(own, other, ints):
    rows, half = ints.shape[0], own.shape[2]
    pairs = 2 * own.shape[0] * own.shape[1]
    tile = tile_of(rows, 512)
    whole = pl.BlockSpec(own.shape, lambda i: (0, 0, 0))
    return pl.pallas_call(
        first_half_kernel,
        grid=(rows // tile,),
        in_specs=[whole, whole, pl.BlockSpec((tile, half), lambda i: (i, 0))],
        out_specs=pl.BlockSpec((pairs, tile), lambda i: (0, i)),
        out_shape=jax.ShapeDtypeStruct((pairs, rows), jnp.float32),
        scratch_shapes=[pltpu.VMEM((pairs, half), jnp.bfloat16)],
        compiler_params=pltpu.CompilerParams(vmem_limit_bytes=VMEM_BYTES),
        cost_estimate=pl.CostEstimate(
            flops=2 * pairs * rows * half, bytes_accessed=2 * rows * half, transcendentals=0
        ),
        name="first_half",
    )(own, other, ints)


def second_half_kernel(steps_ref, own_ref, other_ref, ints_ref, part_ref, out_ref, amps, slots, total, arrived, *, start):
    depth, tile, width = slots.shape
    tiles = part_ref.shape[1] // tile
    steps = steps_ref[0]
    items = tiles * steps

    def fetch(slot, place, step):
        return pltpu.make_async_copy(
            ints_ref.at[
                pl.ds(pl.multiple_of(start + place * tile, tile), tile),
                pl.ds(pl.multiple_of(amps.shape[1] + step * width, 128), width),
            ],
            slots.at[slot],
            arrived.at[slot],
        )

    def following(place, step):
        wraps = step + 1 == steps
        return jnp.where(wraps, place + 1, place), jnp.where(wraps, 0, step + 1)

    ahead = (jnp.int32(0), jnp.int32(0))
    for slot in range(depth - 1):
        @pl.when(slot < items)
        def _(slot=slot, ahead=ahead):
            fetch(slot, *ahead).start()

        ahead = following(*ahead)
    pairs_by_core(own_ref, other_ref, amps)

    def item(index, state):
        place, step, next_place, next_step = state
        slot = lax.rem(index, depth)
        fetch(slot, place, step).wait()

        @pl.when(index + depth - 1 < items)
        def _():
            fetch(lax.rem(index + depth - 1, depth), next_place, next_step).start()

        columns = pl.ds(pl.multiple_of(step * width, 128), width)
        product = lax.dot_general(
            slots[slot], amps[:, columns], CONTRACT_LAST, preferred_element_type=jnp.float32
        )

        @pl.when(step == 0)
        def _():
            total[...] = product

        @pl.when(step > 0)
        def _():
            total[...] += product

        @pl.when(step == steps - 1)
        def _():
            spot = pl.ds(pl.multiple_of(place * tile, 128), tile)
            ladder = total[...].T + part_ref[:, spot]
            own = out_ref.shape[1]
            chips = out_ref.shape[0] // 2
            for core in range(2):
                for chip in range(chips):
                    first = (core * chips + chip) * own
                    out_ref[2 * chip + core, :, spot] = ladder[first : first + own].astype(out_ref.dtype)

        return (*following(place, step), *following(next_place, next_step))

    lax.fori_loop(0, items, item, (jnp.int32(0), jnp.int32(0), *ahead))


def second_half(own, other, ints, part, live_columns, start, count):
    chips, each, half = own.shape
    pairs = 2 * chips * each
    tile = tile_of(count, 1152)
    stripe = 768
    steps = jnp.maximum((live_columns + stripe - 1) // stripe, 1).reshape(1)
    return pl.pallas_call(
        functools.partial(second_half_kernel, start=start),
        grid_spec=pltpu.PrefetchScalarGridSpec(
            num_scalar_prefetch=1,
            grid=(1,),
            in_specs=[
                pl.BlockSpec(own.shape, lambda i, s: (0, 0, 0)),
                pl.BlockSpec(own.shape, lambda i, s: (0, 0, 0)),
                pl.BlockSpec(memory_space=pl.ANY),
                pl.BlockSpec((pairs, count), lambda i, s: (0, start // count)),
            ],
            out_specs=pl.BlockSpec((2 * chips, each, count), lambda i, s: (0, 0, 0)),
            scratch_shapes=[
                pltpu.VMEM((pairs, half), jnp.bfloat16),
                pltpu.VMEM((4, tile, stripe), jnp.bfloat16),
                pltpu.VMEM((tile, pairs), jnp.float32),
                pltpu.SemaphoreType.DMA((4,)),
            ],
        ),
        out_shape=jax.ShapeDtypeStruct((2 * chips, each, count), jnp.bfloat16),
        compiler_params=pltpu.CompilerParams(vmem_limit_bytes=VMEM_BYTES),
        cost_estimate=pl.CostEstimate(
            flops=2 * pairs * count * half, bytes_accessed=2 * count * half, transcendentals=0
        ),
        name="second_half",
    )(steps, own, other, ints, part)


def on_device(devices, t2_amp, ladder_ints, fock_vv, vir_energy, occ_energy, vir_sizes, pair_index):
    irreps = vir_energy.shape[0]
    width = vir_energy.shape[1]
    square = width * width
    half = square // 2
    pair_count = t2_amp.shape[0]
    rows = ladder_ints.shape[0]
    live = jnp.arange(width, dtype=jnp.int32)[None, :] < vir_sizes[:, None]
    pair_live = (live[:, :, None] & live[:, None, :]).reshape(irreps, square)
    block = jnp.where(pair_live[0][None], t2_amp[:, 0, :], 0.0).astype(jnp.bfloat16)
    same_core = [[2 * chip + core for chip in range(devices // 2)] for core in range(2)]
    other_core = [(device, device ^ 1) for device in range(devices)]

    def gathered(part):
        copies = jnp.broadcast_to(part[None], (devices // 2,) + part.shape)
        own = lax.all_to_all(
            copies, "pair", split_axis=0, concat_axis=0, axis_index_groups=same_core
        )
        return own, lax.ppermute(own, "pair", other_core)

    first = gathered(block[:, :half])
    second = gathered(block[:, half:])
    part = first_half(*first, ladder_ints)
    second_live = (vir_sizes[0] - width // 2) * width
    cuts = 2 if rows % 256 == 0 else 1
    pieces = []
    for piece in range(cuts):
        count = rows // cuts
        sent = second_half(*second, ladder_ints, part, second_live, piece * count, count)
        pieces.append(lax.all_to_all(sent, "pair", split_axis=0, concat_axis=0))
    ladder = jnp.concatenate(pieces, axis=2)
    ladder = jnp.swapaxes(ladder, 0, 1).reshape(pair_count, irreps, square).astype(jnp.float32)

    masked = jnp.where(pair_live[None], t2_amp, jnp.zeros_like(t2_amp))
    amps = masked.reshape(pair_count, irreps, width, width)
    fock = jnp.einsum("phac,hcb->phab", amps, fock_vv, precision=lax.Precision.HIGHEST)
    fock = fock + jnp.einsum("hac,phcb->phab", fock_vv, amps, precision=lax.Precision.HIGHEST)
    fock = fock.reshape(pair_count, irreps, square)
    occupied = occ_energy.shape[0]
    matched = pair_index[:, :, None] == jnp.arange(occupied, dtype=jnp.int32)[None, None, :]
    chosen = jnp.sum(
        jnp.where(matched, occ_energy[None, None, :], jnp.zeros_like(occ_energy)[None, None, :]),
        axis=-1,
    )
    vir_pair = (vir_energy[:, :, None] + vir_energy[:, None, :]).reshape(irreps, square)
    denom = vir_pair[None] - (chosen[:, 0] + chosen[:, 1])[:, None, None]
    total = (ladder + fock) / denom
    return jnp.where(pair_live[None], total, jnp.zeros_like(total))


def solution(mesh):
    in_specs = (
        P(("groups", "pair"), None, None),
        P(("groups", "pair"), None),
        P("groups", None, None),
        P("groups", None),
        P("groups"),
        P("groups"),
        P(("groups", "pair"), None),
    )
    out_specs = P(("groups", "pair"), None, None)
    return jax.shard_map(
        functools.partial(on_device, mesh.shape["pair"]),
        mesh=mesh,
        in_specs=in_specs,
        out_specs=out_specs,
        check_vma=False,
    )
```

```python
import functools

import jax
import jax.numpy as jnp
from jax import lax
from jax.experimental import pallas as pl
from jax.experimental.pallas import tpu as pltpu
from jax.sharding import PartitionSpec as P

CONTRACT_LAST = (((1,), (1,)), ((), ()))
VMEM_BYTES = 48 * 1024 * 1024


def tile_of(rows, most):
    for size in range(most - most % 128, 0, -128):
        if rows % size == 0:
            return size
    return rows


def pairs_by_core(own_ref, other_ref, amps):
    core = lax.rem(lax.axis_index("pair"), 2)
    count = own_ref.shape[0] * own_ref.shape[1]
    for ref, place in ((own_ref, core), (other_ref, 1 - core)):
        values = ref[...].astype(jnp.float32).reshape(count, ref.shape[2])
        amps[pl.ds(pl.multiple_of(place * count, count), count), :] = values.astype(amps.dtype)


def ladder_kernel(steps_ref, own_ref, other_ref, ints_ref, out_ref, amps, slots, total, arrived):
    depth, tile, width = slots.shape
    tiles = out_ref.shape[2] // tile
    steps = steps_ref[0]
    items = tiles * steps

    def fetch(slot, place, step):
        return pltpu.make_async_copy(
            ints_ref.at[
                pl.ds(pl.multiple_of(place * tile, tile), tile),
                pl.ds(pl.multiple_of(step * width, 128), width),
            ],
            slots.at[slot],
            arrived.at[slot],
        )

    def following(place, step):
        wraps = step + 1 == steps
        return jnp.where(wraps, place + 1, place), jnp.where(wraps, 0, step + 1)

    ahead = (jnp.int32(0), jnp.int32(0))
    for slot in range(depth - 1):
        @pl.when(slot < items)
        def _(slot=slot, ahead=ahead):
            fetch(slot, *ahead).start()

        ahead = following(*ahead)
    pairs_by_core(own_ref, other_ref, amps)

    def item(index, state):
        place, step, next_place, next_step = state
        slot = lax.rem(index, depth)
        fetch(slot, place, step).wait()

        @pl.when(index + depth - 1 < items)
        def _():
            fetch(lax.rem(index + depth - 1, depth), next_place, next_step).start()

        columns = pl.ds(pl.multiple_of(step * width, 128), width)
        product = lax.dot_general(
            slots[slot], amps[:, columns], CONTRACT_LAST, preferred_element_type=jnp.float32
        )

        @pl.when(step == 0)
        def _():
            total[...] = product

        @pl.when(step > 0)
        def _():
            total[...] += product

        @pl.when(step == steps - 1)
        def _():
            spot = pl.ds(pl.multiple_of(place * tile, 128), tile)
            ladder = total[...].T
            own = out_ref.shape[1]
            chips = out_ref.shape[0] // 2
            for core in range(2):
                for chip in range(chips):
                    first = (core * chips + chip) * own
                    out_ref[2 * chip + core, :, spot] = ladder[first : first + own].astype(out_ref.dtype)

        return (*following(place, step), *following(next_place, next_step))

    lax.fori_loop(0, items, item, (jnp.int32(0), jnp.int32(0), *ahead))


def ladder_rows(own, other, ints, live_columns):
    chips, each, columns = own.shape
    rows = ints.shape[0]
    pairs = 2 * chips * each
    tile = tile_of(rows, 1152)
    stripe = 768
    steps = jnp.maximum((live_columns + stripe - 1) // stripe, 1).reshape(1)
    return pl.pallas_call(
        ladder_kernel,
        grid_spec=pltpu.PrefetchScalarGridSpec(
            num_scalar_prefetch=1,
            grid=(1,),
            in_specs=[
                pl.BlockSpec(own.shape, lambda i, s: (0, 0, 0)),
                pl.BlockSpec(own.shape, lambda i, s: (0, 0, 0)),
                pl.BlockSpec(memory_space=pl.ANY),
            ],
            out_specs=pl.BlockSpec((2 * chips, each, rows), lambda i, s: (0, 0, 0)),
            scratch_shapes=[
                pltpu.VMEM((pairs, columns), jnp.bfloat16),
                pltpu.VMEM((4, tile, stripe), jnp.bfloat16),
                pltpu.VMEM((tile, pairs), jnp.float32),
                pltpu.SemaphoreType.DMA((4,)),
            ],
        ),
        out_shape=jax.ShapeDtypeStruct((2 * chips, each, rows), jnp.bfloat16),
        compiler_params=pltpu.CompilerParams(vmem_limit_bytes=VMEM_BYTES),
        cost_estimate=pl.CostEstimate(
            flops=2 * pairs * rows * columns, bytes_accessed=2 * rows * columns, transcendentals=0
        ),
        name="ladder_rows",
    )(steps, own, other, ints)


def on_device(devices, t2_amp, ladder_ints, fock_vv, vir_energy, occ_energy, vir_sizes, pair_index):
    irreps = vir_energy.shape[0]
    width = vir_energy.shape[1]
    square = width * width
    pair_count = t2_amp.shape[0]
    live = jnp.arange(width, dtype=jnp.int32)[None, :] < vir_sizes[:, None]
    pair_live = (live[:, :, None] & live[:, None, :]).reshape(irreps, square)
    block = jnp.where(pair_live[0][None], t2_amp[:, 0, :], 0.0).astype(jnp.bfloat16)
    same_core = [[2 * chip + core for chip in range(devices // 2)] for core in range(2)]
    other_core = [(device, device ^ 1) for device in range(devices)]

    copies = jnp.broadcast_to(block[None], (devices // 2,) + block.shape)
    own = lax.all_to_all(
        copies, "pair", split_axis=0, concat_axis=0, axis_index_groups=same_core
    )
    masked = jnp.where(pair_live[None], t2_amp, jnp.zeros_like(t2_amp))
    amps = masked.reshape(pair_count, irreps, width, width)
    fock = jnp.einsum("phac,hcb->phab", amps, fock_vv, precision=lax.Precision.HIGHEST)
    own, amps, fock = lax.optimization_barrier((own, amps, fock))
    other = lax.ppermute(own, "pair", other_core)
    sent = ladder_rows(own, other, ladder_ints, vir_sizes[0] * width)
    sent, amps, fock = lax.optimization_barrier((sent, amps, fock))
    ladder = lax.all_to_all(sent, "pair", split_axis=0, concat_axis=0)
    ladder = jnp.swapaxes(ladder, 0, 1).reshape(pair_count, irreps, square).astype(jnp.float32)
    fock = fock + jnp.einsum("hac,phcb->phab", fock_vv, amps, precision=lax.Precision.HIGHEST)
    fock = fock.reshape(pair_count, irreps, square)
    occupied = occ_energy.shape[0]
    matched = pair_index[:, :, None] == jnp.arange(occupied, dtype=jnp.int32)[None, None, :]
    chosen = jnp.sum(
        jnp.where(matched, occ_energy[None, None, :], jnp.zeros_like(occ_energy)[None, None, :]),
        axis=-1,
    )
    vir_pair = (vir_energy[:, :, None] + vir_energy[:, None, :]).reshape(irreps, square)
    denom = vir_pair[None] - (chosen[:, 0] + chosen[:, 1])[:, None, None]
    total = (ladder + fock) / denom
    return jnp.where(pair_live[None], total, jnp.zeros_like(total))


def solution(mesh):
    in_specs = (
        P(("groups", "pair"), None, None),
        P(("groups", "pair"), None),
        P("groups", None, None),
        P("groups", None),
        P("groups"),
        P("groups"),
        P(("groups", "pair"), None),
    )
    out_specs = P(("groups", "pair"), None, None)
    return jax.shard_map(
        functools.partial(on_device, mesh.shape["pair"]),
        mesh=mesh,
        in_specs=in_specs,
        out_specs=out_specs,
        check_vma=False,
    )
```

```python
import functools

import jax
import jax.numpy as jnp
from jax import lax
from jax.experimental import pallas as pl
from jax.experimental.pallas import tpu as pltpu
from jax.sharding import PartitionSpec as P

CONTRACT_LAST = (((1,), (1,)), ((), ()))
VMEM_BYTES = 48 * 1024 * 1024
IN_VMEM = pl.BlockSpec(memory_space=pltpu.VMEM)
IN_SMEM = pl.BlockSpec(memory_space=pltpu.SMEM)
ANYWHERE = pl.BlockSpec(memory_space=pl.ANY)


def tile_of(rows, most):
    for size in range(most - most % 128, 0, -128):
        if rows % size == 0:
            return size
    return rows


def block_kernel(sizes_ref, amps_ref, first_ref, second_ref, *, width):
    columns = amps_ref.shape[2]
    spot = lax.broadcasted_iota(jnp.int32, (1, columns), 1)
    c = ((spot.astype(jnp.float32) + 0.5) * (1.0 / width)).astype(jnp.int32)
    d = spot - c * width
    live = (c < sizes_ref[0]) & (d < sizes_ref[0])
    block = jnp.where(live, amps_ref[:, 0, :], 0.0).astype(jnp.bfloat16)
    half = columns // 2
    for copy in range(first_ref.shape[0]):
        first_ref[copy] = block[:, :half]
    for copy in range(second_ref.shape[0]):
        second_ref[copy] = block[:, half:]


def block_copies(sizes, amps, devices):
    pairs, _, columns = amps.shape
    width = int(columns**0.5)
    half = columns // 2
    return pl.pallas_call(
        functools.partial(block_kernel, width=width),
        in_specs=[IN_SMEM, IN_VMEM],
        out_specs=[IN_VMEM, IN_VMEM],
        out_shape=[
            jax.ShapeDtypeStruct((devices // 2, pairs, half), jnp.bfloat16),
            jax.ShapeDtypeStruct((devices, pairs, half), jnp.bfloat16),
        ],
        compiler_params=pltpu.CompilerParams(vmem_limit_bytes=VMEM_BYTES),
        name="block_copies",
    )(sizes, amps)


def first_kernel(own_ref, other_ref, ints_ref, part_ref, amps, slots, arrived):
    depth, tile, half = slots.shape
    tiles = part_ref.shape[0] // tile

    def fetch(slot, place):
        return pltpu.make_async_copy(
            ints_ref.at[pl.ds(pl.multiple_of(place * tile, tile), tile), pl.ds(0, half)],
            slots.at[slot],
            arrived.at[slot],
        )

    for slot in range(min(depth - 1, tiles)):
        fetch(slot, slot).start()
    core = lax.rem(lax.axis_index("pair"), 2)
    own = own_ref[...].astype(jnp.float32)
    other = other_ref[...].astype(jnp.float32)
    both = [jnp.where(core == 0, own, other), jnp.where(core == 0, other, own)]
    amps[...] = jnp.concatenate(both, axis=1).reshape(amps.shape).astype(amps.dtype)

    def item(place, carry):
        slot = lax.rem(place, depth)
        fetch(slot, place).wait()

        @pl.when(place + depth - 1 < tiles)
        def _():
            fetch(lax.rem(place + depth - 1, depth), place + depth - 1).start()

        part_ref[pl.ds(pl.multiple_of(place * tile, tile), tile), :] = lax.dot_general(
            slots[slot], amps[...], CONTRACT_LAST, preferred_element_type=jnp.float32
        )
        return carry

    lax.fori_loop(0, tiles, item, 0)


def first_half(own, other, ints):
    chips, each, half = own.shape
    pairs = 2 * chips * each
    rows = ints.shape[0]
    tile = tile_of(rows, 384)
    depth = 4
    return pl.pallas_call(
        first_kernel,
        in_specs=[IN_VMEM, IN_VMEM, ANYWHERE],
        out_specs=IN_VMEM,
        out_shape=jax.ShapeDtypeStruct((rows, pairs), jnp.float32),
        scratch_shapes=[
            pltpu.VMEM((pairs, half), jnp.bfloat16),
            pltpu.VMEM((depth, tile, half), jnp.bfloat16),
            pltpu.SemaphoreType.DMA((depth,)),
        ],
        compiler_params=pltpu.CompilerParams(vmem_limit_bytes=VMEM_BYTES),
        cost_estimate=pl.CostEstimate(
            flops=2 * pairs * rows * half, bytes_accessed=2 * rows * half, transcendentals=0
        ),
        name="first_half",
    )(own, other, ints)


def second_kernel(sizes_ref, all_ref, part_ref, ints_ref, out_ref, amps, slots, total, arrived, *, orbitals):
    depth, tile, width = slots.shape
    half = amps.shape[1]
    tiles = part_ref.shape[0] // tile
    columns = (sizes_ref[0] - orbitals // 2) * orbitals
    steps = jnp.int32(1)
    for step in range(1, half // width):
        steps += (columns > step * width).astype(jnp.int32)
    items = tiles * steps

    def fetch(slot, place, step):
        return pltpu.make_async_copy(
            ints_ref.at[
                pl.ds(pl.multiple_of(place * tile, tile), tile),
                pl.ds(pl.multiple_of(half + step * width, 128), width),
            ],
            slots.at[slot],
            arrived.at[slot],
        )

    def following(place, step):
        wraps = step + 1 == steps
        return jnp.where(wraps, place + 1, place), jnp.where(wraps, 0, step + 1)

    ahead = (jnp.int32(0), jnp.int32(0))
    for slot in range(depth - 1):

        @pl.when(slot < items)
        def _(slot=slot, ahead=ahead):
            fetch(slot, *ahead).start()

        ahead = following(*ahead)
    amps[...] = all_ref[...].astype(jnp.float32).reshape(amps.shape).astype(amps.dtype)

    def item(index, state):
        place, step, next_place, next_step = state
        slot = lax.rem(index, depth)
        fetch(slot, place, step).wait()

        @pl.when(index + depth - 1 < items)
        def _():
            fetch(lax.rem(index + depth - 1, depth), next_place, next_step).start()

        product = lax.dot_general(
            slots[slot],
            amps[:, pl.ds(pl.multiple_of(step * width, 128), width)],
            CONTRACT_LAST,
            preferred_element_type=jnp.float32,
        )

        @pl.when(step == 0)
        def _():
            total[...] = product + part_ref[pl.ds(pl.multiple_of(place * tile, tile), tile), :]

        @pl.when(step > 0)
        def _():
            total[...] += product

        @pl.when(step == steps - 1)
        def _():
            spot = pl.ds(pl.multiple_of(place * tile, 128), tile)
            ladder = total[...].T
            own = out_ref.shape[1]
            for device in range(out_ref.shape[0]):
                out_ref[device, :, spot] = ladder[device * own : (device + 1) * own].astype(
                    out_ref.dtype
                )

        return (*following(place, step), *following(next_place, next_step))

    lax.fori_loop(0, items, item, (jnp.int32(0), jnp.int32(0), *ahead))


def second_half(sizes, gathered, part, ints):
    devices, each, half = gathered.shape
    rows, pairs = part.shape
    tile = tile_of(rows, 1152)
    depth = 4
    stripe = half // 6
    return pl.pallas_call(
        functools.partial(second_kernel, orbitals=int((2 * half) ** 0.5)),
        in_specs=[IN_SMEM, IN_VMEM, IN_VMEM, ANYWHERE],
        out_specs=IN_VMEM,
        out_shape=jax.ShapeDtypeStruct((devices, each, rows), jnp.bfloat16),
        scratch_shapes=[
            pltpu.VMEM((pairs, half), jnp.bfloat16),
            pltpu.VMEM((depth, tile, stripe), jnp.bfloat16),
            pltpu.VMEM((tile, pairs), jnp.float32),
            pltpu.SemaphoreType.DMA((depth,)),
        ],
        compiler_params=pltpu.CompilerParams(vmem_limit_bytes=VMEM_BYTES),
        cost_estimate=pl.CostEstimate(
            flops=2 * pairs * rows * half, bytes_accessed=2 * rows * half, transcendentals=0
        ),
        name="second_half",
    )(sizes, gathered, part, ints)


def on_device(devices, t2_amp, ladder_ints, fock_vv, vir_energy, occ_energy, vir_sizes, pair_index):
    irreps = vir_energy.shape[0]
    width = vir_energy.shape[1]
    square = width * width
    pair_count = t2_amp.shape[0]
    same_core = [[2 * chip + core for chip in range(devices // 2)] for core in range(2)]
    other_core = [(device, device ^ 1) for device in range(devices)]
    first, second = block_copies(vir_sizes, t2_amp, devices)
    own = lax.all_to_all(
        first, "pair", split_axis=0, concat_axis=0, axis_index_groups=same_core
    )
    gathered = lax.all_to_all(second, "pair", split_axis=0, concat_axis=0)
    other = lax.ppermute(own, "pair", other_core)
    part = first_half(own, other, ladder_ints)
    sent = second_half(vir_sizes, gathered, part, ladder_ints)

    sent, t2_amp, vir_energy, occ_energy = lax.optimization_barrier(
        (sent, t2_amp, vir_energy, occ_energy)
    )
    ladder = lax.all_to_all(sent, "pair", split_axis=0, concat_axis=0)
    live = jnp.arange(width, dtype=jnp.int32)[None, :] < vir_sizes[:, None]
    pair_live = (live[:, :, None] & live[:, None, :]).reshape(irreps, square)
    masked = jnp.where(pair_live[None], t2_amp, jnp.zeros_like(t2_amp))
    amps = masked.reshape(pair_count, irreps, width, width)
    fock = jnp.einsum("phac,hcb->phab", amps, fock_vv, precision=lax.Precision.HIGHEST)
    fock = fock + jnp.einsum("hac,phcb->phab", fock_vv, amps, precision=lax.Precision.HIGHEST)
    fock = fock.reshape(pair_count, irreps, square)
    occupied = occ_energy.shape[0]
    matched = pair_index[:, :, None] == jnp.arange(occupied, dtype=jnp.int32)[None, None, :]
    chosen = jnp.sum(
        jnp.where(matched, occ_energy[None, None, :], jnp.zeros_like(occ_energy)[None, None, :]),
        axis=-1,
    )
    vir_pair = (vir_energy[:, :, None] + vir_energy[:, None, :]).reshape(irreps, square)
    denom = vir_pair[None] - (chosen[:, 0] + chosen[:, 1])[:, None, None]
    scale = jnp.where(pair_live[None], 1.0 / denom, 0.0)
    ladder, scale, offset = lax.optimization_barrier((ladder, scale, scale * fock))
    ladder = jnp.swapaxes(ladder, 0, 1).reshape(pair_count, irreps, square).astype(jnp.float32)
    return ladder * scale + offset


def solution(mesh):
    in_specs = (
        P(("groups", "pair"), None, None),
        P(("groups", "pair"), None),
        P("groups", None, None),
        P("groups", None),
        P("groups"),
        P("groups"),
        P(("groups", "pair"), None),
    )
    out_specs = P(("groups", "pair"), None, None)
    return jax.shard_map(
        functools.partial(on_device, mesh.shape["pair"]),
        mesh=mesh,
        in_specs=in_specs,
        out_specs=out_specs,
        check_vma=False,
    )
```

```python
import functools

import jax
import jax.numpy as jnp
from jax import lax
from jax.experimental import pallas as pl
from jax.experimental.pallas import tpu as pltpu
from jax.sharding import PartitionSpec as P

CONTRACT_LAST = (((1,), (1,)), ((), ()))
VMEM_BYTES = 48 * 1024 * 1024
IN_VMEM = pl.BlockSpec(memory_space=pltpu.VMEM)
IN_SMEM = pl.BlockSpec(memory_space=pltpu.SMEM)
ANYWHERE = pl.BlockSpec(memory_space=pl.ANY)


def tile_of(rows, most):
    for size in range(most - most % 128, 0, -128):
        if rows % size == 0:
            return size
    return rows


def block_kernel(sizes_ref, amps_ref, copies_ref, *, width):
    columns = amps_ref.shape[2]
    spot = lax.broadcasted_iota(jnp.int32, (1, columns), 1)
    c = ((spot.astype(jnp.float32) + 0.5) * (1.0 / width)).astype(jnp.int32)
    d = spot - c * width
    live = (c < sizes_ref[0]) & (d < sizes_ref[0])
    block = jnp.where(live, amps_ref[:, 0, :], 0.0).astype(jnp.bfloat16)
    for copy in range(copies_ref.shape[0]):
        copies_ref[copy] = block


def block_copies(sizes, amps, chips, width):
    pairs, _, columns = amps.shape
    return pl.pallas_call(
        functools.partial(block_kernel, width=width),
        in_specs=[IN_SMEM, IN_VMEM],
        out_specs=IN_VMEM,
        out_shape=jax.ShapeDtypeStruct((chips, pairs, columns), jnp.bfloat16),
        compiler_params=pltpu.CompilerParams(vmem_limit_bytes=VMEM_BYTES),
        name="block_copies",
    )(sizes, amps)


def ladder_kernel(sizes_ref, own_ref, other_ref, ints_ref, out_ref, amps, slots, arrived, *, orbitals, stripe):
    depth, tile, columns = slots.shape
    tiles = out_ref.shape[2] // tile
    each = out_ref.shape[1]
    live = sizes_ref[0] * orbitals
    least = columns // (2 * stripe)
    most = columns // stripe
    steps = jnp.int32(least)
    for step in range(least, most):
        steps += (live > step * stripe).astype(jnp.int32)

    def fetch(width, slot, place):
        return pltpu.make_async_copy(
            ints_ref.at[pl.ds(pl.multiple_of(place * tile, tile), tile), pl.ds(0, width)],
            slots.at[slot, :, pl.ds(0, width)],
            arrived.at[slot],
        )

    def begin(width):
        for slot in range(min(depth - 1, tiles)):
            fetch(width, slot, slot).start()

    def run(width):
        def item(place, carry):
            slot = lax.rem(place, depth)
            fetch(width, slot, place).wait()

            @pl.when(place + depth - 1 < tiles)
            def _():
                fetch(width, lax.rem(place + depth - 1, depth), place + depth - 1).start()

            ladder = lax.dot_general(
                slots[slot, :, :width],
                amps[:, :width],
                CONTRACT_LAST,
                preferred_element_type=jnp.float32,
            ).T
            spot = pl.ds(pl.multiple_of(place * tile, 128), tile)
            for device in range(out_ref.shape[0]):
                out_ref[device, :, spot] = ladder[device * each : (device + 1) * each].astype(
                    out_ref.dtype
                )
            return carry

        lax.fori_loop(0, tiles, item, 0)

    for count in range(least, most + 1):
        pl.when(steps == count)(functools.partial(begin, count * stripe))
    core = lax.rem(lax.axis_index("pair"), 2)
    own = own_ref[...].astype(jnp.float32)
    other = other_ref[...].astype(jnp.float32)
    both = [jnp.where(core == 0, own, other), jnp.where(core == 0, other, own)]
    amps[...] = jnp.concatenate(both, axis=1).reshape(amps.shape).astype(amps.dtype)
    for count in range(least, most + 1):
        pl.when(steps == count)(functools.partial(run, count * stripe))


def ladder_rows(sizes, own, other, ints, orbitals):
    chips, each, columns = own.shape
    pairs = 2 * chips * each
    rows = ints.shape[0]
    tile = tile_of(rows, 256)
    depth = 4 if tile <= 256 else 3
    return pl.pallas_call(
        functools.partial(ladder_kernel, orbitals=orbitals, stripe=columns // 12),
        in_specs=[IN_SMEM, IN_VMEM, IN_VMEM, ANYWHERE],
        out_specs=IN_VMEM,
        out_shape=jax.ShapeDtypeStruct((2 * chips, each, rows), jnp.bfloat16),
        scratch_shapes=[
            pltpu.VMEM((pairs, columns), jnp.bfloat16),
            pltpu.VMEM((depth, tile, columns), jnp.bfloat16),
            pltpu.SemaphoreType.DMA((depth,)),
        ],
        compiler_params=pltpu.CompilerParams(vmem_limit_bytes=VMEM_BYTES),
        cost_estimate=pl.CostEstimate(
            flops=2 * pairs * rows * columns, bytes_accessed=2 * rows * columns, transcendentals=0
        ),
        name="ladder_rows",
    )(sizes, own, other, ints)


def increment_kernel(ladder_ref, scale_ref, offset_ref, out_ref):
    devices, pairs, rows = ladder_ref.shape
    irreps = out_ref.shape[1]
    each = devices // irreps
    for pair in range(pairs):
        for piece in range(each):
            lines = [
                ladder_ref[irrep * each + piece, pair : pair + 1, :].astype(jnp.float32)
                for irrep in range(irreps)
            ]
            spot = slice(piece * rows, (piece + 1) * rows)
            out_ref[pair, :, spot] = (
                jnp.concatenate(lines, axis=0) * scale_ref[pair, :, spot] + offset_ref[pair, :, spot]
            )


def increments(ladder, scale, offset):
    if ladder.shape[2] % 128 or ladder.shape[0] % scale.shape[1]:
        ladder = jnp.swapaxes(ladder, 0, 1).reshape(scale.shape).astype(jnp.float32)
        return ladder * scale + offset
    return pl.pallas_call(
        increment_kernel,
        in_specs=[IN_VMEM] * 3,
        out_specs=IN_VMEM,
        out_shape=jax.ShapeDtypeStruct(scale.shape, scale.dtype),
        compiler_params=pltpu.CompilerParams(vmem_limit_bytes=VMEM_BYTES),
        name="increments",
    )(ladder, scale, offset)


def on_device(devices, t2_amp, ladder_ints, fock_vv, vir_energy, occ_energy, vir_sizes, pair_index):
    irreps = vir_energy.shape[0]
    width = vir_energy.shape[1]
    square = width * width
    pair_count = t2_amp.shape[0]
    same_core = [[2 * chip + core for chip in range(devices // 2)] for core in range(2)]
    other_core = [(device, device ^ 1) for device in range(devices)]
    copies = block_copies(vir_sizes, t2_amp, devices // 2, width)
    own = lax.all_to_all(
        copies, "pair", split_axis=0, concat_axis=0, axis_index_groups=same_core
    )
    live = jnp.arange(width, dtype=jnp.int32)[None, :] < vir_sizes[:, None]
    pair_live = (live[:, :, None] & live[:, None, :]).reshape(irreps, square)
    masked = jnp.where(pair_live[None], t2_amp, jnp.zeros_like(t2_amp))
    amps = masked.reshape(pair_count, irreps, width, width)
    fock = jnp.einsum("phac,hcb->phab", amps, fock_vv, precision=lax.Precision.HIGHEST)
    fock = fock + jnp.einsum("hac,phcb->phab", fock_vv, amps, precision=lax.Precision.HIGHEST)
    fock = fock.reshape(pair_count, irreps, square)
    own, fock = lax.optimization_barrier((own, fock))
    other = lax.ppermute(own, "pair", other_core)
    sent = ladder_rows(vir_sizes, own, other, ladder_ints, width)

    sent, fock, vir_energy, occ_energy = lax.optimization_barrier(
        (sent, fock, vir_energy, occ_energy)
    )
    ladder = lax.all_to_all(sent, "pair", split_axis=0, concat_axis=0)
    occupied = occ_energy.shape[0]
    matched = pair_index[:, :, None] == jnp.arange(occupied, dtype=jnp.int32)[None, None, :]
    chosen = jnp.sum(
        jnp.where(matched, occ_energy[None, None, :], jnp.zeros_like(occ_energy)[None, None, :]),
        axis=-1,
    )
    vir_pair = (vir_energy[:, :, None] + vir_energy[:, None, :]).reshape(irreps, square)
    denom = vir_pair[None] - (chosen[:, 0] + chosen[:, 1])[:, None, None]
    scale = jnp.where(pair_live[None], 1.0 / denom, 0.0)
    ladder, scale, offset = lax.optimization_barrier((ladder, scale, scale * fock))
    return increments(ladder, scale, offset)


def solution(mesh):
    in_specs = (
        P(("groups", "pair"), None, None),
        P(("groups", "pair"), None),
        P("groups", None, None),
        P("groups", None),
        P("groups"),
        P("groups"),
        P(("groups", "pair"), None),
    )
    out_specs = P(("groups", "pair"), None, None)
    return jax.shard_map(
        functools.partial(on_device, mesh.shape["pair"]),
        mesh=mesh,
        in_specs=in_specs,
        out_specs=out_specs,
        check_vma=False,
    )
```

```python
import functools

import jax
import jax.numpy as jnp
from jax import lax
from jax.experimental import pallas as pl
from jax.experimental.pallas import tpu as pltpu
from jax.sharding import PartitionSpec as P

CONTRACT_LAST = (((1,), (1,)), ((), ()))
RING_BYTES = 48 * 1024 * 1024
IN_VMEM = pl.BlockSpec(memory_space=pltpu.VMEM)
IN_SMEM = pl.BlockSpec(memory_space=pltpu.SMEM)
ANYWHERE = pl.BlockSpec(memory_space=pl.ANY)


def tile_of(rows, most):
    for size in range(most - most % 128, 0, -128):
        if rows % size == 0:
            return size
    return rows


def block_kernel(sizes_ref, amps_ref, first_ref, second_ref, *, width):
    columns = amps_ref.shape[2]
    half = columns // 2
    spot = lax.broadcasted_iota(jnp.int32, (1, columns), 1)
    c = ((spot.astype(jnp.float32) + 0.5) * (1.0 / width)).astype(jnp.int32)
    d = spot - c * width
    live = (c < sizes_ref[0]) & (d < sizes_ref[0])
    block = jnp.where(live, amps_ref[:, 0, :], 0.0).astype(jnp.bfloat16)
    for copy in range(first_ref.shape[0]):
        first_ref[copy] = block[:, :half]
    for copy in range(second_ref.shape[0]):
        second_ref[copy] = block[:, half:]


def block_copies(sizes, amps, devices, width):
    pairs, _, columns = amps.shape
    half = columns // 2
    return pl.pallas_call(
        functools.partial(block_kernel, width=width),
        in_specs=[IN_SMEM, IN_VMEM],
        out_specs=[IN_VMEM, IN_VMEM],
        out_shape=[
            jax.ShapeDtypeStruct((devices // 2, pairs, half), jnp.bfloat16),
            jax.ShapeDtypeStruct((devices, pairs, half), jnp.bfloat16),
        ],
        compiler_params=pltpu.CompilerParams(vmem_limit_bytes=4 * 1024 * 1024),
        name="block_copies",
    )(sizes, amps)


def first_kernel(own_ref, other_ref, ints_ref, part_ref, blocks, amps, slots, arrived, landed):
    depth, tile, half = slots.shape
    tiles = part_ref.shape[1] // tile

    def fetch(slot, place):
        return pltpu.make_async_copy(
            ints_ref.at[pl.ds(pl.multiple_of(place * tile, tile), tile), pl.ds(0, half)],
            slots.at[slot],
            arrived.at[slot],
        )

    copies = [
        pltpu.make_async_copy(ref, blocks.at[k], landed.at[k])
        for k, ref in enumerate((own_ref, other_ref))
    ]
    for copy in copies:
        copy.start()
    for place in range(min(depth - 1, tiles)):
        fetch(place, place).start()
    for copy in copies:
        copy.wait()
    core = lax.rem(lax.axis_index("pair"), 2)
    own = blocks[0].astype(jnp.float32)
    other = blocks[1].astype(jnp.float32)
    both = [jnp.where(core == 0, own, other), jnp.where(core == 0, other, own)]
    amps[...] = jnp.concatenate(both, axis=1).reshape(amps.shape).astype(amps.dtype)

    def item(place, carry):
        slot = lax.rem(place, depth)
        fetch(slot, place).wait()

        @pl.when(place + depth - 1 < tiles)
        def _():
            fetch(lax.rem(place + depth - 1, depth), place + depth - 1).start()

        part_ref[:, pl.ds(pl.multiple_of(place * tile, 128), tile)] = lax.dot_general(
            slots[slot], amps[...], CONTRACT_LAST, preferred_element_type=jnp.float32
        ).T
        return carry

    lax.fori_loop(0, tiles, item, 0)


def first_half(own, other, ints, tile):
    chips, each, half = own.shape
    pairs = 2 * chips * each
    rows = ints.shape[0]
    depth = 4
    return pl.pallas_call(
        first_kernel,
        in_specs=[ANYWHERE, ANYWHERE, ANYWHERE],
        out_specs=IN_VMEM,
        out_shape=jax.ShapeDtypeStruct((pairs, rows), jnp.float32),
        scratch_shapes=[
            pltpu.VMEM((2, chips, each, half), jnp.bfloat16),
            pltpu.VMEM((pairs, half), jnp.bfloat16),
            pltpu.VMEM((depth, tile, half), jnp.bfloat16),
            pltpu.SemaphoreType.DMA((depth,)),
            pltpu.SemaphoreType.DMA((2,)),
        ],
        compiler_params=pltpu.CompilerParams(vmem_limit_bytes=RING_BYTES),
        cost_estimate=pl.CostEstimate(
            flops=2 * pairs * rows * half, bytes_accessed=2 * rows * half, transcendentals=0
        ),
        name="first_half",
    )(own, other, ints)


def second_kernel(sizes_ref, all_ref, part_ref, ints_ref, out_ref, blocks, amps, slots, arrived, landed, *, orbitals):
    depth, tile, half = slots.shape
    tiles = part_ref.shape[1] // tile
    each = out_ref.shape[1]
    most = 6
    stripe = half // most
    columns = (sizes_ref[0] - orbitals // 2) * orbitals
    steps = jnp.int32(1)
    for step in range(1, most):
        steps += (columns > step * stripe).astype(jnp.int32)

    def fetch(width, slot, place):
        return pltpu.make_async_copy(
            ints_ref.at[pl.ds(pl.multiple_of(place * tile, tile), tile), pl.ds(half, width)],
            slots.at[slot, :, pl.ds(0, width)],
            arrived.at[slot],
        )

    def begin(width):
        for place in range(min(depth - 1, tiles)):
            fetch(width, place, place).start()

    def store(spot, ints, width):
        ladder = lax.dot_general(
            ints, amps[:, :width], CONTRACT_LAST, preferred_element_type=jnp.float32
        )
        ladder = ladder.T + part_ref[:, spot]
        for device in range(out_ref.shape[0]):
            out_ref[device, :, spot] = ladder[device * each : (device + 1) * each].astype(
                out_ref.dtype
            )

    def run(width):
        def item(place, carry):
            slot = lax.rem(place, depth)
            fetch(width, slot, place).wait()

            @pl.when(place + depth - 1 < tiles)
            def _():
                fetch(width, lax.rem(place + depth - 1, depth), place + depth - 1).start()

            store(pl.ds(pl.multiple_of(place * tile, 128), tile), slots[slot, :, :width], width)
            return carry

        lax.fori_loop(0, tiles, item, 0)

    copy = pltpu.make_async_copy(all_ref, blocks, landed)
    copy.start()
    for count in range(1, most + 1):
        pl.when(steps == count)(functools.partial(begin, count * stripe))
    copy.wait()
    amps[...] = blocks[...].astype(jnp.float32).reshape(amps.shape).astype(amps.dtype)
    for count in range(1, most + 1):
        pl.when(steps == count)(functools.partial(run, count * stripe))


def second_half(sizes, gathered, part, ints, tile, orbitals):
    devices, each, half = gathered.shape
    pairs, rows = part.shape
    depth = 4
    return pl.pallas_call(
        functools.partial(second_kernel, orbitals=orbitals),
        in_specs=[IN_SMEM, ANYWHERE, IN_VMEM, ANYWHERE],
        out_specs=IN_VMEM,
        out_shape=jax.ShapeDtypeStruct((devices, each, rows), jnp.bfloat16),
        scratch_shapes=[
            pltpu.VMEM((devices, each, half), jnp.bfloat16),
            pltpu.VMEM((pairs, half), jnp.bfloat16),
            pltpu.VMEM((depth, tile, half), jnp.bfloat16),
            pltpu.SemaphoreType.DMA((depth,)),
            pltpu.SemaphoreType.DMA,
        ],
        compiler_params=pltpu.CompilerParams(vmem_limit_bytes=RING_BYTES),
        cost_estimate=pl.CostEstimate(
            flops=2 * pairs * rows * half, bytes_accessed=2 * rows * half, transcendentals=0
        ),
        name="second_half",
    )(sizes, gathered, part, ints)


def increment_kernel(ladder_ref, scale_ref, offset_ref, out_ref):
    devices, pairs, rows = ladder_ref.shape
    irreps = out_ref.shape[1]
    each = devices // irreps
    for pair in range(pairs):
        for piece in range(each):
            lines = [
                ladder_ref[irrep * each + piece, pair : pair + 1, :].astype(jnp.float32)
                for irrep in range(irreps)
            ]
            spot = slice(piece * rows, (piece + 1) * rows)
            out_ref[pair, :, spot] = (
                jnp.concatenate(lines, axis=0) * scale_ref[pair, :, spot] + offset_ref[pair, :, spot]
            )


def increments(ladder, scale, offset):
    if ladder.shape[2] % 128 or ladder.shape[0] % scale.shape[1]:
        ladder = jnp.swapaxes(ladder, 0, 1).reshape(scale.shape).astype(jnp.float32)
        return ladder * scale + offset
    return pl.pallas_call(
        increment_kernel,
        in_specs=[IN_VMEM] * 3,
        out_specs=IN_VMEM,
        out_shape=jax.ShapeDtypeStruct(scale.shape, scale.dtype),
        compiler_params=pltpu.CompilerParams(vmem_limit_bytes=16 * 1024 * 1024),
        name="increments",
    )(ladder, scale, offset)


def on_device(devices, t2_amp, ladder_ints, fock_vv, vir_energy, occ_energy, vir_sizes, pair_index):
    irreps = vir_energy.shape[0]
    width = vir_energy.shape[1]
    square = width * width
    pair_count = t2_amp.shape[0]
    same_core = [[2 * chip + core for chip in range(devices // 2)] for core in range(2)]
    other_core = [(device, device ^ 1) for device in range(devices)]
    rows = ladder_ints.shape[0]
    tile = tile_of(rows, 384)
    first, second = block_copies(vir_sizes, t2_amp, devices, width)
    own = lax.all_to_all(
        first, "pair", split_axis=0, concat_axis=0, axis_index_groups=same_core
    )
    own, second = lax.optimization_barrier((own, second))
    other = lax.ppermute(own, "pair", other_core)
    gathered = lax.all_to_all(second, "pair", split_axis=0, concat_axis=0)
    part = first_half(own, other, ladder_ints, tile)
    sent = second_half(vir_sizes, gathered, part, ladder_ints, tile, width)

    sent, t2_amp, vir_energy, occ_energy = lax.optimization_barrier(
        (sent, t2_amp, vir_energy, occ_energy)
    )
    ladder = lax.all_to_all(sent, "pair", split_axis=0, concat_axis=0)
    live = jnp.arange(width, dtype=jnp.int32)[None, :] < vir_sizes[:, None]
    pair_live = (live[:, :, None] & live[:, None, :]).reshape(irreps, square)
    masked = jnp.where(pair_live[None], t2_amp, jnp.zeros_like(t2_amp))
    amps = masked.reshape(pair_count, irreps, width, width)
    fock = jnp.einsum("phac,hcb->phab", amps, fock_vv, precision=lax.Precision.HIGHEST)
    fock = fock + jnp.einsum("hac,phcb->phab", fock_vv, amps, precision=lax.Precision.HIGHEST)
    fock = fock.reshape(pair_count, irreps, square)
    occupied = occ_energy.shape[0]
    matched = pair_index[:, :, None] == jnp.arange(occupied, dtype=jnp.int32)[None, None, :]
    chosen = jnp.sum(
        jnp.where(matched, occ_energy[None, None, :], jnp.zeros_like(occ_energy)[None, None, :]),
        axis=-1,
    )
    vir_pair = (vir_energy[:, :, None] + vir_energy[:, None, :]).reshape(irreps, square)
    denom = vir_pair[None] - (chosen[:, 0] + chosen[:, 1])[:, None, None]
    scale = jnp.where(pair_live[None], 1.0 / denom, 0.0)
    ladder, scale, offset = lax.optimization_barrier((ladder, scale, scale * fock))
    return increments(ladder, scale, offset)


def solution(mesh):
    in_specs = (
        P(("groups", "pair"), None, None),
        P(("groups", "pair"), None),
        P("groups", None, None),
        P("groups", None),
        P("groups"),
        P("groups"),
        P(("groups", "pair"), None),
    )
    out_specs = P(("groups", "pair"), None, None)
    return jax.shard_map(
        functools.partial(on_device, mesh.shape["pair"]),
        mesh=mesh,
        in_specs=in_specs,
        out_specs=out_specs,
        check_vma=False,
    )
```

```python
import functools

import jax
import jax.numpy as jnp
from jax import lax
from jax.experimental import pallas as pl
from jax.experimental.pallas import tpu as pltpu
from jax.sharding import PartitionSpec as P

CONTRACT_LAST = (((1,), (1,)), ((), ()))
RING_BYTES = 48 * 1024 * 1024
IN_VMEM = pl.BlockSpec(memory_space=pltpu.VMEM)
IN_SMEM = pl.BlockSpec(memory_space=pltpu.SMEM)
ANYWHERE = pl.BlockSpec(memory_space=pl.ANY)


def tile_of(rows, most):
    for size in range(most - most % 128, 0, -128):
        if rows % size == 0:
            return size
    return rows


def block_kernel(sizes_ref, amps_ref, first_ref, second_ref, sizes, amps, arrived, *, width):
    copies = [
        pltpu.make_async_copy(sizes_ref, sizes, arrived.at[0]),
        pltpu.make_async_copy(amps_ref, amps, arrived.at[1]),
    ]
    for copy in copies:
        copy.start()
    columns = amps_ref.shape[2]
    half = columns // 2
    spot = lax.broadcasted_iota(jnp.int32, (1, columns), 1)
    c = ((spot.astype(jnp.float32) + 0.5) * (1.0 / width)).astype(jnp.int32)
    d = spot - c * width
    for copy in copies:
        copy.wait()
    live = (c < sizes[0]) & (d < sizes[0])
    block = jnp.where(live, amps[:, 0, :], 0.0).astype(jnp.bfloat16)
    for copy in range(first_ref.shape[0]):
        first_ref[copy] = block[:, :half]
    for copy in range(second_ref.shape[0]):
        second_ref[copy] = block[:, half:]


def block_copies(sizes, amps, devices, width):
    pairs, _, columns = amps.shape
    half = columns // 2
    return pl.pallas_call(
        functools.partial(block_kernel, width=width),
        in_specs=[ANYWHERE, ANYWHERE],
        out_specs=[IN_VMEM, IN_VMEM],
        out_shape=[
            jax.ShapeDtypeStruct((devices // 2, pairs, half), jnp.bfloat16),
            jax.ShapeDtypeStruct((devices, pairs, half), jnp.bfloat16),
        ],
        scratch_shapes=[
            pltpu.SMEM(sizes.shape, sizes.dtype),
            pltpu.VMEM(amps.shape, amps.dtype),
            pltpu.SemaphoreType.DMA((2,)),
        ],
        compiler_params=pltpu.CompilerParams(vmem_limit_bytes=63 * 1024 * 1024),
        name="block_copies",
    )(sizes, amps)


def first_kernel(own_ref, other_ref, ints_ref, part_ref, blocks, amps, slots, arrived, landed):
    depth, tile, half = slots.shape
    tiles = part_ref.shape[1] // tile

    def fetch(slot, place):
        return pltpu.make_async_copy(
            ints_ref.at[pl.ds(pl.multiple_of(place * tile, tile), tile), pl.ds(0, half)],
            slots.at[slot],
            arrived.at[slot],
        )

    core = lax.rem(lax.axis_index("pair"), 2)
    copies = [
        pltpu.make_async_copy(own_ref, blocks.at[core], landed.at[0]),
        pltpu.make_async_copy(other_ref, blocks.at[1 - core], landed.at[1]),
    ]
    for copy in copies:
        copy.start()
    for place in range(min(depth - 1, tiles)):
        fetch(place, place).start()
    for copy in copies:
        copy.wait()
    both = [blocks[core].astype(jnp.float32) for core in range(2)]
    amps[...] = jnp.concatenate(both, axis=1).reshape(amps.shape).astype(amps.dtype)

    def item(place, carry):
        slot = lax.rem(place, depth)
        fetch(slot, place).wait()

        @pl.when(place + depth - 1 < tiles)
        def _():
            fetch(lax.rem(place + depth - 1, depth), place + depth - 1).start()

        part_ref[:, pl.ds(pl.multiple_of(place * tile, 128), tile)] = lax.dot_general(
            slots[slot], amps[...], CONTRACT_LAST, preferred_element_type=jnp.float32
        ).T
        return carry

    lax.fori_loop(0, tiles, item, 0)


def first_half(own, other, ints, tile):
    chips, each, half = own.shape
    pairs = 2 * chips * each
    rows = ints.shape[0]
    depth = 4
    return pl.pallas_call(
        first_kernel,
        in_specs=[ANYWHERE, ANYWHERE, ANYWHERE],
        out_specs=IN_VMEM,
        out_shape=jax.ShapeDtypeStruct((pairs, rows), jnp.float32),
        scratch_shapes=[
            pltpu.VMEM((2, chips, each, half), jnp.bfloat16),
            pltpu.VMEM((pairs, half), jnp.bfloat16),
            pltpu.VMEM((depth, tile, half), jnp.bfloat16),
            pltpu.SemaphoreType.DMA((depth,)),
            pltpu.SemaphoreType.DMA((2,)),
        ],
        compiler_params=pltpu.CompilerParams(vmem_limit_bytes=RING_BYTES),
        cost_estimate=pl.CostEstimate(
            flops=2 * pairs * rows * half, bytes_accessed=2 * rows * half, transcendentals=0
        ),
        name="first_half",
    )(own, other, ints)


def second_kernel(sizes_ref, all_ref, part_ref, ints_ref, out_ref, blocks, amps, slots, arrived, landed, *, orbitals):
    depth, tile, half = slots.shape
    tiles = part_ref.shape[1] // tile
    each = out_ref.shape[1]
    most = 6
    stripe = half // most
    columns = (sizes_ref[0] - orbitals // 2) * orbitals
    steps = jnp.int32(1)
    for step in range(1, most):
        steps += (columns > step * stripe).astype(jnp.int32)

    def fetch(width, slot, place):
        return pltpu.make_async_copy(
            ints_ref.at[pl.ds(pl.multiple_of(place * tile, tile), tile), pl.ds(half, width)],
            slots.at[slot, :, pl.ds(0, width)],
            arrived.at[slot],
        )

    def begin(width):
        for place in range(min(depth - 1, tiles)):
            fetch(width, place, place).start()

    def store(spot, ints, width):
        ladder = lax.dot_general(
            ints, amps[:, :width], CONTRACT_LAST, preferred_element_type=jnp.float32
        )
        ladder = ladder.T + part_ref[:, spot]
        for device in range(out_ref.shape[0]):
            out_ref[device, :, spot] = ladder[device * each : (device + 1) * each].astype(
                out_ref.dtype
            )

    def run(width):
        def item(place, carry):
            slot = lax.rem(place, depth)
            fetch(width, slot, place).wait()

            @pl.when(place + depth - 1 < tiles)
            def _():
                fetch(width, lax.rem(place + depth - 1, depth), place + depth - 1).start()

            store(pl.ds(pl.multiple_of(place * tile, 128), tile), slots[slot, :, :width], width)
            return carry

        lax.fori_loop(0, tiles, item, 0)

    copy = pltpu.make_async_copy(all_ref, blocks, landed)
    copy.start()
    for count in range(1, most + 1):
        pl.when(steps == count)(functools.partial(begin, count * stripe))
    copy.wait()
    amps[...] = blocks[...].astype(jnp.float32).reshape(amps.shape).astype(amps.dtype)
    for count in range(1, most + 1):
        pl.when(steps == count)(functools.partial(run, count * stripe))


def second_half(sizes, gathered, part, ints, tile, orbitals):
    devices, each, half = gathered.shape
    pairs, rows = part.shape
    depth = 4
    return pl.pallas_call(
        functools.partial(second_kernel, orbitals=orbitals),
        in_specs=[IN_SMEM, ANYWHERE, IN_VMEM, ANYWHERE],
        out_specs=IN_VMEM,
        out_shape=jax.ShapeDtypeStruct((devices, each, rows), jnp.bfloat16),
        scratch_shapes=[
            pltpu.VMEM((devices, each, half), jnp.bfloat16),
            pltpu.VMEM((pairs, half), jnp.bfloat16),
            pltpu.VMEM((depth, tile, half), jnp.bfloat16),
            pltpu.SemaphoreType.DMA((depth,)),
            pltpu.SemaphoreType.DMA,
        ],
        compiler_params=pltpu.CompilerParams(vmem_limit_bytes=RING_BYTES),
        cost_estimate=pl.CostEstimate(
            flops=2 * pairs * rows * half, bytes_accessed=2 * rows * half, transcendentals=0
        ),
        name="second_half",
    )(sizes, gathered, part, ints)


def increment_kernel(occupied_ref, ladder_ref, fock_ref, virtual_ref, out_ref):
    devices, pairs, rows = ladder_ref.shape
    irreps = out_ref.shape[1]
    each = devices // irreps
    for pair in range(pairs):
        for piece in range(each):
            lines = [
                ladder_ref[irrep * each + piece, pair : pair + 1, :].astype(jnp.float32)
                for irrep in range(irreps)
            ]
            spot = slice(piece * rows, (piece + 1) * rows)
            total = jnp.concatenate(lines, axis=0) + fock_ref[pair, :, spot]
            out_ref[pair, :, spot] = total / (virtual_ref[:, spot] - occupied_ref[pair])


def increments(ladder, fock, virtual, occupied):
    if ladder.shape[2] % 128 or ladder.shape[0] % fock.shape[1]:
        ladder = jnp.swapaxes(ladder, 0, 1).reshape(fock.shape).astype(jnp.float32)
        return (ladder + fock) / (virtual[None] - occupied[:, None, None])
    return pl.pallas_call(
        increment_kernel,
        in_specs=[IN_SMEM] + [IN_VMEM] * 3,
        out_specs=IN_VMEM,
        out_shape=jax.ShapeDtypeStruct(fock.shape, fock.dtype),
        compiler_params=pltpu.CompilerParams(vmem_limit_bytes=16 * 1024 * 1024),
        name="increments",
    )(occupied, ladder, fock, virtual)


def on_device(devices, t2_amp, ladder_ints, fock_vv, vir_energy, occ_energy, vir_sizes, pair_index):
    irreps = vir_energy.shape[0]
    width = vir_energy.shape[1]
    square = width * width
    pair_count = t2_amp.shape[0]
    same_core = [[2 * chip + core for chip in range(devices // 2)] for core in range(2)]
    other_core = [(device, device ^ 1) for device in range(devices)]
    rows = ladder_ints.shape[0]
    tile = tile_of(rows, 384)
    first, second = block_copies(vir_sizes, t2_amp, devices, width)
    own = lax.all_to_all(
        first, "pair", split_axis=0, concat_axis=0, axis_index_groups=same_core
    )
    live = jnp.arange(width, dtype=jnp.int32)[None, :] < vir_sizes[:, None]
    pair_live = (live[:, :, None] & live[:, None, :]).reshape(irreps, square)
    masked = jnp.where(pair_live[None], t2_amp, jnp.zeros_like(t2_amp))
    amps = masked.reshape(pair_count, irreps, width, width)
    own, second, amps = lax.optimization_barrier((own, second, amps))
    other = lax.ppermute(own, "pair", other_core)
    gathered = lax.all_to_all(second, "pair", split_axis=0, concat_axis=0)
    part = first_half(own, other, ladder_ints, tile)
    sent = second_half(vir_sizes, gathered, part, ladder_ints, tile, width)

    sent, amps, vir_energy, occ_energy = lax.optimization_barrier(
        (sent, amps, vir_energy, occ_energy)
    )
    ladder = lax.all_to_all(sent, "pair", split_axis=0, concat_axis=0)
    fock = jnp.einsum("phac,hcb->phab", amps, fock_vv, precision=lax.Precision.HIGHEST)
    fock = fock + jnp.einsum("hac,phcb->phab", fock_vv, amps, precision=lax.Precision.HIGHEST)
    fock = fock.reshape(pair_count, irreps, square)
    occupied = occ_energy.shape[0]
    matched = pair_index[:, :, None] == jnp.arange(occupied, dtype=jnp.int32)[None, None, :]
    chosen = jnp.sum(
        jnp.where(matched, occ_energy[None, None, :], jnp.zeros_like(occ_energy)[None, None, :]),
        axis=-1,
    )
    virtual = (vir_energy[:, :, None] + vir_energy[:, None, :]).reshape(irreps, square)
    virtual = jnp.where(pair_live, virtual, jnp.inf)
    ladder, fock, virtual, chosen = lax.optimization_barrier(
        (ladder, fock, virtual, chosen[:, 0] + chosen[:, 1])
    )
    return increments(ladder, fock, virtual, chosen)


def solution(mesh):
    in_specs = (
        P(("groups", "pair"), None, None),
        P(("groups", "pair"), None),
        P("groups", None, None),
        P("groups", None),
        P("groups"),
        P("groups"),
        P(("groups", "pair"), None),
    )
    out_specs = P(("groups", "pair"), None, None)
    return jax.shard_map(
        functools.partial(on_device, mesh.shape["pair"]),
        mesh=mesh,
        in_specs=in_specs,
        out_specs=out_specs,
        check_vma=False,
    )
```

```python
import functools

import jax
import jax.numpy as jnp
from jax import lax
from jax.experimental import pallas as pl
from jax.experimental.pallas import tpu as pltpu
from jax.sharding import PartitionSpec as P

CONTRACT_LAST = (((1,), (1,)), ((), ()))
VMEM_BYTES = 48 * 1024 * 1024
IN_VMEM = pl.BlockSpec(memory_space=pltpu.VMEM)
IN_SMEM = pl.BlockSpec(memory_space=pltpu.SMEM)
ANYWHERE = pl.BlockSpec(memory_space=pl.ANY)


def tile_of(rows, most):
    for size in range(most - most % 128, 0, -128):
        if rows % size == 0:
            return size
    return rows


def block_kernel(sizes_ref, amps_ref, copies_ref, sizes, amps, arrived, *, width):
    arrivals = [
        pltpu.make_async_copy(sizes_ref, sizes, arrived.at[0]),
        pltpu.make_async_copy(amps_ref, amps, arrived.at[1]),
    ]
    for arrival in arrivals:
        arrival.start()
    spot = lax.broadcasted_iota(jnp.int32, (1, amps_ref.shape[2]), 1)
    c = ((spot.astype(jnp.float32) + 0.5) * (1.0 / width)).astype(jnp.int32)
    d = spot - c * width
    for arrival in arrivals:
        arrival.wait()
    live = (c < sizes[0]) & (d < sizes[0])
    block = jnp.where(live, amps[:, 0, :], 0.0).astype(jnp.bfloat16)
    for copy in range(copies_ref.shape[0]):
        copies_ref[copy] = block


def block_copies(sizes, amps, chips, width):
    pairs, _, columns = amps.shape
    return pl.pallas_call(
        functools.partial(block_kernel, width=width),
        in_specs=[ANYWHERE, ANYWHERE],
        out_specs=IN_VMEM,
        out_shape=jax.ShapeDtypeStruct((chips, pairs, columns), jnp.bfloat16),
        scratch_shapes=[
            pltpu.SMEM(sizes.shape, sizes.dtype),
            pltpu.VMEM(amps.shape, amps.dtype),
            pltpu.SemaphoreType.DMA((2,)),
        ],
        compiler_params=pltpu.CompilerParams(vmem_limit_bytes=63 * 1024 * 1024),
        name="block_copies",
    )(sizes, amps)


def ladder_kernel(sizes_ref, own_ref, other_ref, ints_ref, out_ref, amps, slots, total, arrived, *, orbitals, stripe):
    depth, tile, columns = slots.shape
    tiles = out_ref.shape[2] // tile
    each = out_ref.shape[1]
    live = sizes_ref[0] * orbitals
    least = columns // (2 * stripe)
    most = columns // stripe
    steps = jnp.int32(least)
    for step in range(least, most):
        steps += (live > step * stripe).astype(jnp.int32)

    def fetch(width, slot, place):
        return pltpu.make_async_copy(
            ints_ref.at[pl.ds(pl.multiple_of(place * tile, tile), tile), pl.ds(0, width)],
            slots.at[slot, :, pl.ds(0, width)],
            arrived.at[slot],
        )

    def begin(width):
        for slot in range(min(depth - 1, tiles)):
            fetch(width, slot, slot).start()

    def store(place):
        ladder = total[...].T
        spot = pl.ds(pl.multiple_of(place * tile, 128), tile)
        for device in range(out_ref.shape[0]):
            out_ref[device, :, spot] = ladder[device * each : (device + 1) * each].astype(
                out_ref.dtype
            )

    def run(width):
        def item(place, carry):
            slot = lax.rem(place, depth)
            fetch(width, slot, place).wait()

            @pl.when(place + depth - 1 < tiles)
            def _():
                fetch(width, lax.rem(place + depth - 1, depth), place + depth - 1).start()

            store(jnp.maximum(place - 1, 0))
            total[...] = lax.dot_general(
                slots[slot, :, :width],
                amps[:, :width],
                CONTRACT_LAST,
                preferred_element_type=jnp.float32,
            )
            return carry

        lax.fori_loop(0, tiles, item, 0)

    for count in range(least, most + 1):
        pl.when(steps == count)(functools.partial(begin, count * stripe))
    core = lax.rem(lax.axis_index("pair"), 2)
    own = own_ref[...].astype(jnp.float32)
    other = other_ref[...].astype(jnp.float32)
    both = [jnp.where(core == 0, own, other), jnp.where(core == 0, other, own)]
    amps[...] = jnp.concatenate(both, axis=1).reshape(amps.shape).astype(amps.dtype)
    total[...] = jnp.zeros_like(total)
    for count in range(least, most + 1):
        pl.when(steps == count)(functools.partial(run, count * stripe))
    store(tiles - 1)


def ladder_rows(sizes, own, other, ints, orbitals):
    chips, each, columns = own.shape
    pairs = 2 * chips * each
    rows = ints.shape[0]
    tile = tile_of(rows, 256)
    depth = 4 if tile <= 256 else 3
    return pl.pallas_call(
        functools.partial(ladder_kernel, orbitals=orbitals, stripe=columns // 12),
        in_specs=[IN_SMEM, IN_VMEM, IN_VMEM, ANYWHERE],
        out_specs=IN_VMEM,
        out_shape=jax.ShapeDtypeStruct((2 * chips, each, rows), jnp.bfloat16),
        scratch_shapes=[
            pltpu.VMEM((pairs, columns), jnp.bfloat16),
            pltpu.VMEM((depth, tile, columns), jnp.bfloat16),
            pltpu.VMEM((tile, pairs), jnp.float32),
            pltpu.SemaphoreType.DMA((depth,)),
        ],
        compiler_params=pltpu.CompilerParams(vmem_limit_bytes=VMEM_BYTES),
        cost_estimate=pl.CostEstimate(
            flops=2 * pairs * rows * columns, bytes_accessed=2 * rows * columns, transcendentals=0
        ),
        name="ladder_rows",
    )(sizes, own, other, ints)


def increment_kernel(ladder_ref, scale_ref, offset_ref, out_ref):
    devices, pairs, rows = ladder_ref.shape
    irreps = out_ref.shape[1]
    each = devices // irreps
    for pair in range(pairs):
        for piece in range(each):
            lines = [
                ladder_ref[irrep * each + piece, pair : pair + 1, :].astype(jnp.float32)
                for irrep in range(irreps)
            ]
            spot = slice(piece * rows, (piece + 1) * rows)
            out_ref[pair, :, spot] = (
                jnp.concatenate(lines, axis=0) * scale_ref[pair, :, spot] + offset_ref[pair, :, spot]
            )


def increments(ladder, scale, offset):
    if ladder.shape[2] % 128 or ladder.shape[0] % scale.shape[1]:
        ladder = jnp.swapaxes(ladder, 0, 1).reshape(scale.shape).astype(jnp.float32)
        return ladder * scale + offset
    return pl.pallas_call(
        increment_kernel,
        in_specs=[IN_VMEM] * 3,
        out_specs=IN_VMEM,
        out_shape=jax.ShapeDtypeStruct(scale.shape, scale.dtype),
        compiler_params=pltpu.CompilerParams(vmem_limit_bytes=VMEM_BYTES),
        name="increments",
    )(ladder, scale, offset)


def on_device(devices, t2_amp, ladder_ints, fock_vv, vir_energy, occ_energy, vir_sizes, pair_index):
    irreps = vir_energy.shape[0]
    width = vir_energy.shape[1]
    square = width * width
    pair_count = t2_amp.shape[0]
    same_core = [[2 * chip + core for chip in range(devices // 2)] for core in range(2)]
    other_core = [(device, device ^ 1) for device in range(devices)]
    copies = block_copies(vir_sizes, t2_amp, devices // 2, width)
    own = lax.all_to_all(
        copies, "pair", split_axis=0, concat_axis=0, axis_index_groups=same_core
    )
    live = jnp.arange(width, dtype=jnp.int32)[None, :] < vir_sizes[:, None]
    pair_live = (live[:, :, None] & live[:, None, :]).reshape(irreps, square)
    masked = jnp.where(pair_live[None], t2_amp, jnp.zeros_like(t2_amp))
    amps = masked.reshape(pair_count, irreps, width, width)
    fock = jnp.einsum("phac,hcb->phab", amps, fock_vv, precision=lax.Precision.HIGHEST)
    fock = fock + jnp.einsum("hac,phcb->phab", fock_vv, amps, precision=lax.Precision.HIGHEST)
    fock = fock.reshape(pair_count, irreps, square)
    own, fock = lax.optimization_barrier((own, fock))
    other = lax.ppermute(own, "pair", other_core)
    sent = ladder_rows(vir_sizes, own, other, ladder_ints, width)

    sent, fock, vir_energy, occ_energy = lax.optimization_barrier(
        (sent, fock, vir_energy, occ_energy)
    )
    ladder = lax.all_to_all(sent, "pair", split_axis=0, concat_axis=0)
    occupied = occ_energy.shape[0]
    matched = pair_index[:, :, None] == jnp.arange(occupied, dtype=jnp.int32)[None, None, :]
    chosen = jnp.sum(
        jnp.where(matched, occ_energy[None, None, :], jnp.zeros_like(occ_energy)[None, None, :]),
        axis=-1,
    )
    vir_pair = (vir_energy[:, :, None] + vir_energy[:, None, :]).reshape(irreps, square)
    denom = vir_pair[None] - (chosen[:, 0] + chosen[:, 1])[:, None, None]
    scale = jnp.where(pair_live[None], 1.0 / denom, 0.0)
    ladder, scale, offset = lax.optimization_barrier((ladder, scale, scale * fock))
    return increments(ladder, scale, offset)


def solution(mesh):
    in_specs = (
        P(("groups", "pair"), None, None),
        P(("groups", "pair"), None),
        P("groups", None, None),
        P("groups", None),
        P("groups"),
        P("groups"),
        P(("groups", "pair"), None),
    )
    out_specs = P(("groups", "pair"), None, None)
    return jax.shard_map(
        functools.partial(on_device, mesh.shape["pair"]),
        mesh=mesh,
        in_specs=in_specs,
        out_specs=out_specs,
        check_vma=False,
    )
```

```python
import functools

import jax
import jax.numpy as jnp
from jax import lax
from jax.experimental import pallas as pl
from jax.experimental.pallas import tpu as pltpu
from jax.sharding import PartitionSpec as P

CONTRACT_LAST = (((1,), (1,)), ((), ()))
VMEM_BYTES = 48 * 1024 * 1024
IN_VMEM = pl.BlockSpec(memory_space=pltpu.VMEM)
IN_SMEM = pl.BlockSpec(memory_space=pltpu.SMEM)
ANYWHERE = pl.BlockSpec(memory_space=pl.ANY)


def tile_of(rows, most):
    for size in range(most - most % 128, 0, -128):
        if rows % size == 0:
            return size
    return rows


def block_kernel(sizes_ref, amps_ref, copies_ref, sizes, amps, arrived, *, width):
    arrivals = [
        pltpu.make_async_copy(sizes_ref, sizes, arrived.at[0]),
        pltpu.make_async_copy(amps_ref, amps, arrived.at[1]),
    ]
    for arrival in arrivals:
        arrival.start()
    spot = lax.broadcasted_iota(jnp.int32, (1, amps_ref.shape[2]), 1)
    c = ((spot.astype(jnp.float32) + 0.5) * (1.0 / width)).astype(jnp.int32)
    d = spot - c * width
    for arrival in arrivals:
        arrival.wait()
    live = (c < sizes[0]) & (d < sizes[0])
    block = jnp.where(live, amps[:, 0, :], 0.0).astype(jnp.bfloat16)
    for copy in range(copies_ref.shape[0]):
        copies_ref[copy] = block


def block_copies(sizes, amps, chips, width):
    pairs, _, columns = amps.shape
    return pl.pallas_call(
        functools.partial(block_kernel, width=width),
        in_specs=[ANYWHERE, ANYWHERE],
        out_specs=IN_VMEM,
        out_shape=jax.ShapeDtypeStruct((chips, pairs, columns), jnp.bfloat16),
        scratch_shapes=[
            pltpu.SMEM(sizes.shape, sizes.dtype),
            pltpu.VMEM(amps.shape, amps.dtype),
            pltpu.SemaphoreType.DMA((2,)),
        ],
        compiler_params=pltpu.CompilerParams(vmem_limit_bytes=63 * 1024 * 1024),
        name="block_copies",
    )(sizes, amps)


def head_kernel(ints_ref, head_ref, arrived):
    copy = pltpu.make_async_copy(ints_ref.at[pl.ds(0, head_ref.shape[0])], head_ref, arrived)
    copy.start()
    copy.wait()


def head_of(ints, rows):
    columns = ints.shape[1]
    return pl.pallas_call(
        head_kernel,
        in_specs=[ANYWHERE],
        out_specs=IN_VMEM,
        out_shape=pltpu.VMEM((rows, columns), ints.dtype),
        scratch_shapes=[pltpu.SemaphoreType.DMA],
        compiler_params=pltpu.CompilerParams(vmem_limit_bytes=4 * 1024 * 1024),
        cost_estimate=pl.CostEstimate(
            flops=0, bytes_accessed=4 * rows * columns, transcendentals=0
        ),
        name="head_of_integrals",
    )(ints)


def ladder_kernel(sizes_ref, own_ref, other_ref, head_ref, ints_ref, out_ref, amps, slots, total, arrived, *, orbitals, stripe):
    depth, tile, columns = slots.shape
    tiles = out_ref.shape[2] // tile
    each = out_ref.shape[1]
    live = sizes_ref[0] * orbitals
    least = columns // (2 * stripe)
    most = columns // stripe
    steps = jnp.int32(least)
    for step in range(least, most):
        steps += (live > step * stripe).astype(jnp.int32)

    def fetch(width, slot, place):
        return pltpu.make_async_copy(
            ints_ref.at[pl.ds(pl.multiple_of(place * tile, tile), tile), pl.ds(0, width)],
            slots.at[slot, :, pl.ds(0, width)],
            arrived.at[slot],
        )

    def begin(width):
        for place in range(1, min(depth, tiles)):
            fetch(width, place % depth, place).start()

    def store(place):
        ladder = total[...].T
        spot = pl.ds(pl.multiple_of(place * tile, 128), tile)
        for device in range(out_ref.shape[0]):
            out_ref[device, :, spot] = ladder[device * each : (device + 1) * each].astype(
                out_ref.dtype
            )

    def run(width):
        def item(place, carry):
            slot = lax.rem(place, depth)
            fetch(width, slot, place).wait()

            @pl.when(place + depth - 1 < tiles)
            def _():
                fetch(width, lax.rem(place + depth - 1, depth), place + depth - 1).start()

            store(place - 1)
            total[...] = lax.dot_general(
                slots[slot, :, :width],
                amps[:, :width],
                CONTRACT_LAST,
                preferred_element_type=jnp.float32,
            )
            return carry

        total[...] = lax.dot_general(
            head_ref[:, :width],
            amps[:, :width],
            CONTRACT_LAST,
            preferred_element_type=jnp.float32,
        )
        lax.fori_loop(1, tiles, item, 0)

    for count in range(least, most + 1):
        pl.when(steps == count)(functools.partial(begin, count * stripe))
    core = lax.rem(lax.axis_index("pair"), 2)
    own = own_ref[...].astype(jnp.float32)
    other = other_ref[...].astype(jnp.float32)
    both = [jnp.where(core == 0, own, other), jnp.where(core == 0, other, own)]
    amps[...] = jnp.concatenate(both, axis=1).reshape(amps.shape).astype(amps.dtype)
    for count in range(least, most + 1):
        pl.when(steps == count)(functools.partial(run, count * stripe))
    store(tiles - 1)


def ladder_rows(sizes, own, other, head, ints, orbitals):
    chips, each, columns = own.shape
    pairs = 2 * chips * each
    rows = ints.shape[0]
    tile = head.shape[0]
    depth = 4 if tile <= 256 else 3
    need = 2 * depth * tile * columns + 12 * pairs * columns + 4 * 1024 * 1024
    return pl.pallas_call(
        functools.partial(ladder_kernel, orbitals=orbitals, stripe=columns // 12),
        in_specs=[IN_SMEM, IN_VMEM, IN_VMEM, IN_VMEM, ANYWHERE],
        out_specs=IN_VMEM,
        out_shape=jax.ShapeDtypeStruct((2 * chips, each, rows), jnp.bfloat16),
        scratch_shapes=[
            pltpu.VMEM((pairs, columns), jnp.bfloat16),
            pltpu.VMEM((depth, tile, columns), jnp.bfloat16),
            pltpu.VMEM((tile, pairs), jnp.float32),
            pltpu.SemaphoreType.DMA((depth,)),
        ],
        compiler_params=pltpu.CompilerParams(vmem_limit_bytes=min(VMEM_BYTES, need)),
        cost_estimate=pl.CostEstimate(
            flops=2 * pairs * rows * columns, bytes_accessed=2 * rows * columns, transcendentals=0
        ),
        name="ladder_rows",
    )(sizes, own, other, head, ints)


def increment_kernel(ladder_ref, scale_ref, offset_ref, out_ref):
    devices, pairs, rows = ladder_ref.shape
    irreps = out_ref.shape[1]
    each = devices // irreps
    for pair in range(pairs):
        for piece in range(each):
            lines = [
                ladder_ref[irrep * each + piece, pair : pair + 1, :].astype(jnp.float32)
                for irrep in range(irreps)
            ]
            spot = slice(piece * rows, (piece + 1) * rows)
            out_ref[pair, :, spot] = (
                jnp.concatenate(lines, axis=0) * scale_ref[pair, :, spot] + offset_ref[pair, :, spot]
            )


def increments(ladder, scale, offset):
    if ladder.shape[2] % 128 or ladder.shape[0] % scale.shape[1]:
        ladder = jnp.swapaxes(ladder, 0, 1).reshape(scale.shape).astype(jnp.float32)
        return ladder * scale + offset
    return pl.pallas_call(
        increment_kernel,
        in_specs=[IN_VMEM] * 3,
        out_specs=IN_VMEM,
        out_shape=jax.ShapeDtypeStruct(scale.shape, scale.dtype),
        compiler_params=pltpu.CompilerParams(vmem_limit_bytes=VMEM_BYTES),
        name="increments",
    )(ladder, scale, offset)


def on_device(devices, t2_amp, ladder_ints, fock_vv, vir_energy, occ_energy, vir_sizes, pair_index):
    irreps = vir_energy.shape[0]
    width = vir_energy.shape[1]
    square = width * width
    pair_count = t2_amp.shape[0]
    same_core = [[2 * chip + core for chip in range(devices // 2)] for core in range(2)]
    other_core = [(device, device ^ 1) for device in range(devices)]
    copies = block_copies(vir_sizes, t2_amp, devices // 2, width)
    own = lax.all_to_all(
        copies, "pair", split_axis=0, concat_axis=0, axis_index_groups=same_core
    )
    live = jnp.arange(width, dtype=jnp.int32)[None, :] < vir_sizes[:, None]
    pair_live = (live[:, :, None] & live[:, None, :]).reshape(irreps, square)
    masked = jnp.where(pair_live[None], t2_amp, jnp.zeros_like(t2_amp))
    amps = masked.reshape(pair_count, irreps, width, width)
    fock = jnp.einsum("phac,hcb->phab", amps, fock_vv, precision=lax.Precision.HIGHEST)
    fock = fock + jnp.einsum("hac,phcb->phab", fock_vv, amps, precision=lax.Precision.HIGHEST)
    fock = fock.reshape(pair_count, irreps, square)
    own, fock, ladder_ints = lax.optimization_barrier((own, fock, ladder_ints))
    other = lax.ppermute(own, "pair", other_core)
    head = head_of(ladder_ints, tile_of(ladder_ints.shape[0], 256))
    sent = ladder_rows(vir_sizes, own, other, head, ladder_ints, width)

    sent, fock, vir_energy, occ_energy = lax.optimization_barrier(
        (sent, fock, vir_energy, occ_energy)
    )
    ladder = lax.all_to_all(sent, "pair", split_axis=0, concat_axis=0)
    occupied = occ_energy.shape[0]
    matched = pair_index[:, :, None] == jnp.arange(occupied, dtype=jnp.int32)[None, None, :]
    chosen = jnp.sum(
        jnp.where(matched, occ_energy[None, None, :], jnp.zeros_like(occ_energy)[None, None, :]),
        axis=-1,
    )
    vir_pair = (vir_energy[:, :, None] + vir_energy[:, None, :]).reshape(irreps, square)
    denom = vir_pair[None] - (chosen[:, 0] + chosen[:, 1])[:, None, None]
    scale = jnp.where(pair_live[None], 1.0 / denom, 0.0)
    ladder, scale, offset = lax.optimization_barrier((ladder, scale, scale * fock))
    return increments(ladder, scale, offset)


def solution(mesh):
    in_specs = (
        P(("groups", "pair"), None, None),
        P(("groups", "pair"), None),
        P("groups", None, None),
        P("groups", None),
        P("groups"),
        P("groups"),
        P(("groups", "pair"), None),
    )
    out_specs = P(("groups", "pair"), None, None)
    return jax.shard_map(
        functools.partial(on_device, mesh.shape["pair"]),
        mesh=mesh,
        in_specs=in_specs,
        out_specs=out_specs,
        check_vma=False,
    )
```
